32 devices in a mesh: dp: 4 (over y, x), mp: 8 (over z, core).
Axes of the slice: x: 2, y: 2, z: 4, core: 2. Of those that a mesh axis runs over, the one named last changes fastest.
Arguments:
- grads_a: bfloat16 [4, 4, 1792, 576], P('dp', None, 'mp'), may hold values from -360 to 360
- momentum_a: float32 [7168, 576], P(('dp', 'mp')), may hold values from -6 to 6
- weights_a: bfloat16 [7168, 576], P(('dp', 'mp')), may hold values from -6 to 6
- up_gradient_parts: bfloat16 [4, 4, 4096, 512], P('dp', None, 'mp'), may hold values from -360 to 360
- up_momentum_buffer: float32 [16384, 512], P(('dp', 'mp')), may hold values from -6 to 6
- up_weight_before: bfloat16 [16384, 512], P(('dp', 'mp')), may hold values from -6 to 6
Outputs:
- new_weight_a: bfloat16 [4, 1792, 576], P(None, 'mp')
- new_momentum_a: float32 [7168, 576], P(('dp', 'mp'))
- update_a: float32 [7168, 576], P(('dp', 'mp'))
- new_weight_b: bfloat16 [4, 4096, 512], P(None, 'mp')
- new_momentum_b: float32 [16384, 512], P(('dp', 'mp'))
- up_scaled_update: float32 [16384, 512], P(('dp', 'mp'))
The draws below stay inside these ranges and needn't reach their ends.
All inputs are finite; a program needn't handle non-finite values.
Results may differ from the reference program's by a relative error of at most 0.008.
Values may be sent and summed in bfloat16 or wider, within the bound.
A program may use at most 64 MiB of HBM per device.

```python
import math
import jax
import jax.numpy as jnp
from jax import lax

D = 7168
KV = 576
LATENT_WIDTH = 512
KEY_VALUE_ROWS = 16384
ITERS = 3
N_DP = 4


def draw_row_count(key, total_rows, columns):
    first, second, third = jax.random.split(key, 3)
    shape = (N_DP, N_DP, total_rows // N_DP, columns)
    row_count = jnp.arange(total_rows, dtype=jnp.float32).reshape(1, N_DP, total_rows // N_DP, 1)
    rising = 1.0 + 2.0 * row_count / total_rows
    row_scale = jnp.exp(jax.random.uniform(second, (1, N_DP, total_rows // N_DP, 1), jnp.float32) * math.log(10.0))
    col_scale = jnp.exp(jax.random.uniform(third, (1, 1, 1, columns), jnp.float32) * math.log(10.0))
    noise = jnp.clip(jax.random.normal(first, shape, jnp.float32), -6.0, 6.0)
    base = noise
    return (base * rising * row_scale * col_scale * 0.2).astype(jnp.bfloat16)


def draw_grads_a(key, part):
    key = jax.random.fold_in(key, 1)
    return draw_row_count(key, D, KV)


def draw_up_gradient_parts(key, part):
    key = jax.random.fold_in(key, 2)
    return draw_row_count(key, KEY_VALUE_ROWS, LATENT_WIDTH)


def level_of(own_key, shape, pieces, smallest, high):
    level, own = 1.0, jax.random.fold_in(own_key, 6)
    for dim, blocks in pieces:
        heights = jnp.exp(jax.random.uniform(jax.random.fold_in(own, dim), (blocks,), jnp.float32, smallest / len(pieces), high / len(pieces)))
        level = level * jnp.repeat(heights, shape[dim] // blocks).reshape([-1 if axis == dim else 1 for axis in range(len(shape))])
    return level


def gaussian(stream_key, dims, deviation, most, pieces=(), kind=jnp.bfloat16):
    entries = jax.random.normal(stream_key, dims, jnp.float32) * deviation
    if len(pieces) > 0:
        entries = level_of(stream_key, dims, pieces, -0.22, 0.18) * entries
    return jnp.clip(entries, min=-most, max=most).astype(kind)


def setup_inputs(seed: int = 0) -> dict:
    splits = jax.random.split(jax.random.key(seed), 7)
    return {
        "grads_a": draw_grads_a(jax.random.fold_in(splits[6], 71), 0),
        "momentum_a": gaussian(splits[1], (D, KV), 1.0, 6.0, ((0, 32),), jnp.float32),
        "weights_a": gaussian(splits[2], (D, KV), 1.0, 6.0, ((0, 32),)),
        "up_gradient_parts": draw_up_gradient_parts(jax.random.fold_in(splits[6], 71), 0),
        "up_momentum_buffer": gaussian(splits[4], (KEY_VALUE_ROWS, LATENT_WIDTH), 1.0, 6.0, ((0, 32),), jnp.float32),
        "up_weight_before": gaussian(splits[5], (KEY_VALUE_ROWS, LATENT_WIDTH), 1.0, 6.0, ((0, 32),)),
    }


COEF_A = 3.4445
COEF_B = -4.775
COEF_C = 2.0315
MOMENT = 0.95
RATE = 0.2
DECAY = 0.1
EPSILON = 1e-07
PRECISE = lax.Precision.HIGHEST

def orthogonal_update_step(grads, momentum, weights, total_rows, columns):
    summed = lax.optimization_barrier(jnp.sum(grads.astype(jnp.float32), axis=0)).reshape(total_rows, columns)
    new_momentum = MOMENT * momentum + summed
    direction = summed + MOMENT * new_momentum
    norm_value = jnp.sqrt(jnp.sum(direction * direction))
    iterate = direction / (norm_value + EPSILON)
    for step in range(ITERS):
        gram_matrix = jnp.dot(iterate.T, iterate, precision=PRECISE, preferred_element_type=jnp.float32)
        squared = jnp.dot(gram_matrix, gram_matrix, precision=PRECISE, preferred_element_type=jnp.float32)
        polynomial = COEF_B * gram_matrix + COEF_C * squared
        iterate = COEF_A * iterate + jnp.dot(iterate, polynomial, precision=PRECISE, preferred_element_type=jnp.float32)
    update = 0.2 * math.sqrt(total_rows) * iterate
    new_weight = (weights.astype(jnp.float32) * (1.0 - RATE * DECAY) - RATE * update).astype(jnp.bfloat16)
    return (new_weight.reshape(N_DP, total_rows // N_DP, columns), new_momentum, update)

def reference(grads_a, momentum_a, weights_a, up_gradient_parts, up_momentum_buffer, up_weight_before):
    weight_a, state_a, update_a = orthogonal_update_step(grads_a, momentum_a, weights_a, D, KV)
    up_weight_matrix, up_optimizer_state, up_scaled_update = orthogonal_update_step(up_gradient_parts, up_momentum_buffer, up_weight_before, KEY_VALUE_ROWS, LATENT_WIDTH)
    return (weight_a, state_a, update_a, up_weight_matrix, up_optimizer_state, up_scaled_update)
```

```python
import functools
import math

import jax
import jax.numpy as jnp
from jax import lax
from jax.experimental import pallas as pl
from jax.experimental.pallas import tpu as pltpu
from jax.sharding import PartitionSpec as P

D = 7168
KEY_VALUE_ROWS = 16384
ITERS = 3

COEF_A = 3.4445
COEF_B = -4.775
COEF_C = 2.0315
MOMENT = 0.95
RATE = 0.2
DECAY = 0.1
EPSILON = 1e-07
MESH = pl.DeviceIdType.MESH
F32 = jnp.float32
BF16 = jnp.bfloat16
BLOCK = 128


def block_list(columns):
    count = -(-columns // BLOCK)
    return [(i, j) for i in range(count) for j in range(i, count)]


def split(value):
    high = value.astype(BF16)
    return high, (value - high.astype(F32)).astype(BF16)


def partners(dp, mp):
    d, m = lax.axis_index("dp"), lax.axis_index("mp")
    core = lax.rem(m, 2)
    sibling = (d, m + 1 - 2 * core)
    group = [(lax.rem(d + r, dp), m) for r in range(1, dp)]
    line = [(d, lax.rem(m + 2 * r, mp)) for r in range(1, mp // 2)]
    return d, m, core, sibling, group, line


def greet(others):
    barrier = pltpu.get_barrier_semaphore()
    for other in others:
        pl.semaphore_signal(barrier, inc=1, device_id=other, device_id_type=MESH)
    pl.semaphore_wait(barrier, len(others))


def remote(src, dst, send, recv, target):
    return pltpu.make_async_remote_copy(
        src_ref=src, dst_ref=dst, send_sem=send, recv_sem=recv, device_id=target, device_id_type=MESH
    )


def gather_rows(start, size):
    return pl.ds(pl.multiple_of(start, 8), size)


def reduce_kernel(
    dp, mp, total,
    grads_a, grads_b, mom_a, mom_b,
    new_a, new_b, dir_a, dir_b, gram_a, gram_b,
    own_a, own_b, got_a, got_b, wide_a, pack, half, quarter, part, red, quart_recv, part_recv,
    own_sem, rs_send, rs_recv, core_sem, dp_send, dp_recv, line_send, line_recv, line_send2, line_recv2,
    dp_send2, dp_recv2,
):
    d, m, core, sibling, group, line = partners(dp, mp)
    z = m // 2
    zn = mp // 2
    half_rows = total // 2
    quarter_rows = half_rows // dp
    part_rows = quarter_rows // zn
    locals_ = [
        pltpu.make_async_copy(grads_b.at[0, d], own_b, own_sem.at[0]),
        pltpu.make_async_copy(grads_a.at[0, d], own_a, own_sem.at[1]),
    ]
    for copy in locals_:
        copy.start()
    greet([sibling] + group + line)
    scatter = [[], []]
    for which, (grads, got) in enumerate(((grads_b, got_b), (grads_a, got_a))):
        for r in range(1, dp):
            target = group[r - 1]
            copy = remote(
                grads.at[0, target[0]], got.at[r - 1],
                rs_send.at[which, r - 1], rs_recv.at[which, r - 1], target,
            )
            copy.start()
            scatter[which].append(copy)

    used = (len(block_list(gram_a.shape[0])) + len(block_list(gram_b.shape[0]))) * BLOCK
    if total > used:
        pack[pl.ds(used, total - used), :] = jnp.zeros((total - used, BLOCK), F32)
    offset_a = len(block_list(gram_b.shape[0])) * BLOCK

    for which, (own, got, mom, new, direction) in enumerate(
        ((own_b, got_b, mom_b, new_b, dir_b), (own_a, got_a, mom_a, new_a, dir_a))
    ):
        locals_[which].wait()
        for copy in scatter[which]:
            copy.wait_recv()
        summed = own[...].astype(F32)
        for r in range(dp - 1):
            summed = summed + got[r].astype(F32)
        state = MOMENT * mom[...] + summed
        new[...] = state
        value = summed + MOMENT * state
        direction[...] = value
        columns = value.shape[1]
        count = -(-columns // BLOCK)
        if columns % BLOCK:
            wide_a[...] = jnp.zeros(wide_a.shape, F32)
            wide_a[:, :columns] = value
            value = wide_a[...]
        high, low = split(value)
        at = offset_a if which else 0
        for i in range(count):
            left = slice(i * BLOCK, (i + 1) * BLOCK)
            right = slice(i * BLOCK, count * BLOCK)

            def product(x, y):
                return lax.dot_general(x, y, (((0,), (0,)), ((), ())), preferred_element_type=F32)

            row = (
                product(high[:, left], high[:, right])
                + product(high[:, left], low[:, right])
                + product(low[:, left], high[:, right])
            )
            for j in range(count - i):
                pack[at : at + BLOCK, :] = row[:, j * BLOCK : (j + 1) * BLOCK]
                at += BLOCK
    core_copy = remote(
        pack.at[gather_rows((1 - core) * half_rows, half_rows)], half, core_sem.at[0], core_sem.at[1], sibling
    )
    core_copy.start()
    core_copy.wait()
    half[...] = half[...] + pack[gather_rows(core * half_rows, half_rows), :]
    copies = []
    for r in range(1, dp):
        target = group[r - 1]
        copy = remote(
            half.at[gather_rows(target[0] * quarter_rows, quarter_rows)], quart_recv.at[r - 1],
            dp_send.at[r - 1], dp_recv.at[r - 1], target,
        )
        copy.start()
        copies.append(copy)
    value = half[gather_rows(d * quarter_rows, quarter_rows), :]
    for r, copy in enumerate(copies):
        copy.wait_recv()
        value = value + quart_recv[r]
    quarter[...] = value
    line_copies = []
    for r in range(1, zn):
        target = line[r - 1]
        copy = remote(
            quarter.at[gather_rows((target[1] // 2) * part_rows, part_rows)], part_recv.at[r - 1],
            line_send.at[r - 1], line_recv.at[r - 1], target,
        )
        copy.start()
        line_copies.append(copy)
    value = quarter[gather_rows(z * part_rows, part_rows), :]
    for r, copy in enumerate(line_copies):
        copy.wait_recv()
        value = value + part_recv[r]
    my_quarter = core * half_rows + d * quarter_rows
    my_part = my_quarter + z * part_rows
    red[gather_rows(my_part, part_rows), :] = value
    back = []
    for r in range(1, zn):
        spot = red.at[gather_rows(my_part, part_rows)]
        copy = remote(spot, spot, line_send2.at[r - 1], line_recv2.at[r - 1], line[r - 1])
        copy.start()
        back.append(copy)
    for copy in back:
        copy.wait_recv()
    back_dp = []
    for r in range(1, dp):
        spot = red.at[gather_rows(my_quarter, quarter_rows)]
        copy = remote(spot, spot, dp_send2.at[r - 1], dp_recv2.at[r - 1], group[r - 1])
        copy.start()
        back_dp.append(copy)
    for copy in back_dp:
        copy.wait_recv()
    spot = red.at[gather_rows(core * half_rows, half_rows)]
    core_back = remote(spot, spot, core_sem.at[2], core_sem.at[3], sibling)
    core_back.start()
    for copy in scatter[0] + scatter[1] + copies + line_copies + back + back_dp:
        copy.wait_send()
    core_back.wait()
    at = 0
    for gram in (gram_b, gram_a):
        columns = gram.shape[0]
        for i, j in block_list(columns):
            block = red[at : at + BLOCK, :]
            at += BLOCK
            rows_end = min((i + 1) * BLOCK, columns)
            cols_end = min((j + 1) * BLOCK, columns)
            high_rows, wide = rows_end - i * BLOCK, cols_end - j * BLOCK
            gram[i * BLOCK : rows_end, j * BLOCK : cols_end] = block[:high_rows, :wide]
            if i != j:
                gram[j * BLOCK : cols_end, i * BLOCK : rows_end] = block.T[:wide, :high_rows]


def reduce_call(dp, mp, grads_a, grads_b, mom_a, mom_b):
    ra, ca = mom_a.shape
    rb, cb = mom_b.shape
    unit = 8 * dp * mp
    used = (len(block_list(ca)) + len(block_list(cb))) * BLOCK
    total = -(-used // unit) * unit
    zn = mp // 2
    half_rows = total // 2
    quarter_rows = half_rows // dp
    part_rows = quarter_rows // zn
    vmem = pl.BlockSpec(memory_space=pltpu.VMEM)
    hbm = pl.BlockSpec(memory_space=pl.ANY)
    shape = jax.ShapeDtypeStruct
    sem = pltpu.SemaphoreType.DMA
    wide = -(-ca // BLOCK) * BLOCK
    return pl.pallas_call(
        functools.partial(reduce_kernel, dp, mp, total),
        out_shape=[
            shape((ra, ca), F32), shape((rb, cb), F32),
            shape((ra, ca), F32), shape((rb, cb), F32),
            shape((ca, ca), F32), shape((cb, cb), F32),
        ],
        in_specs=[hbm, hbm, vmem, vmem],
        out_specs=[vmem] * 6,
        scratch_shapes=[
            pltpu.VMEM((ra, ca), BF16),
            pltpu.VMEM((rb, cb), BF16),
            pltpu.VMEM((dp - 1, ra, ca), BF16),
            pltpu.VMEM((dp - 1, rb, cb), BF16),
            pltpu.VMEM((ra, wide), F32),
            pltpu.VMEM((total, BLOCK), F32),
            pltpu.VMEM((half_rows, BLOCK), F32),
            pltpu.VMEM((quarter_rows, BLOCK), F32),
            pltpu.VMEM((part_rows, BLOCK), F32),
            pltpu.VMEM((total, BLOCK), F32),
            pltpu.VMEM((dp - 1, quarter_rows, BLOCK), F32),
            pltpu.VMEM((zn - 1, part_rows, BLOCK), F32),
            sem((2,)),
            sem((2, dp - 1)),
            sem((2, dp - 1)),
            sem((4,)),
            sem((dp - 1,)),
            sem((dp - 1,)),
            sem((zn - 1,)),
            sem((zn - 1,)),
            sem((zn - 1,)),
            sem((zn - 1,)),
            sem((dp - 1,)),
            sem((dp - 1,)),
        ],
        compiler_params=pltpu.CompilerParams(
            collective_id=0, has_side_effects=True, vmem_limit_bytes=40 * 2**20
        ),
    )(grads_a, grads_b, mom_a, mom_b)


def spread_kernel(dp, rows_a, rows_b, out_a, out_b, own_sem, send, recv):
    d, m = lax.axis_index("dp"), lax.axis_index("mp")
    low, high = lax.rem(d, 2), d // 2
    near = (d + 1 - 2 * low, m)
    far = (lax.rem(d + 2, 4), m)
    mine = [
        pltpu.make_async_copy(rows_b, out_b.at[d], own_sem.at[0]),
        pltpu.make_async_copy(rows_a, out_a.at[d], own_sem.at[1]),
    ]
    for copy in mine:
        copy.start()
    greet([near, far])
    first = {}
    for which, (rows, out) in enumerate(((rows_b, out_b), (rows_a, out_a))):
        for side, target in enumerate((near, far)):
            copy = remote(rows, out.at[d], send.at[which, side], recv.at[which, side], target)
            copy.start()
            first[which, side] = copy
    later = []
    for which, (rows, out) in enumerate(((rows_b, out_b), (rows_a, out_a))):
        count = rows.shape[0]
        cut = count // 2 // 16 * 16
        for side, (source, target, start, size) in enumerate(
            ((near[0], far, 0, cut), (far[0], near, cut, count - cut))
        ):
            first[which, side].wait_recv()
            if size:
                spot = out.at[source] if size == count else out.at[source, pl.ds(start, size)]
                copy = remote(spot, spot, send.at[which, 2 + side], recv.at[which, 2 + side], target)
                copy.start()
                later.append(copy)
    for copy in mine:
        copy.wait()
    for copy in first.values():
        copy.wait_send()
    for copy in later:
        copy.wait()


def spread_call(dp, rows_a, rows_b):
    hbm = pl.BlockSpec(memory_space=pl.ANY)
    sem = pltpu.SemaphoreType.DMA
    return pl.pallas_call(
        functools.partial(spread_kernel, dp),
        out_shape=[
            jax.ShapeDtypeStruct((dp,) + rows_a.shape, BF16),
            jax.ShapeDtypeStruct((dp,) + rows_b.shape, BF16),
        ],
        in_specs=[hbm, hbm],
        out_specs=[hbm, hbm],
        scratch_shapes=[sem((2,)), sem((2, 4)), sem((2, 4))],
        compiler_params=pltpu.CompilerParams(collective_id=1, has_side_effects=True),
    )(rows_a, rows_b)


def times(x, y):
    return jnp.dot(x, y, precision=lax.Precision.HIGH, preferred_element_type=F32)


def orthogonal(direction, gram):
    scale = 1.0 / (jnp.sqrt(jnp.trace(gram)) + EPSILON)
    iterate = direction * scale
    gram = gram * scale * scale
    for step in range(ITERS):
        poly = COEF_B * gram + COEF_C * times(gram, gram)
        if step < ITERS - 1:
            inner = COEF_A * gram + times(gram, poly)
            gram = COEF_A * inner + times(poly, inner)
        iterate = COEF_A * iterate + times(iterate, poly)
    return iterate


def local(dp, mp, grads_a, momentum_a, weights_a, up_gradient_parts, up_momentum_buffer, up_weight_before):
    new_a, new_b, dir_a, dir_b, gram_a, gram_b = reduce_call(
        dp, mp, grads_a, up_gradient_parts, momentum_a, up_momentum_buffer
    )
    update_a = 0.2 * math.sqrt(D) * orthogonal(dir_a, gram_a)
    update_b = 0.2 * math.sqrt(KEY_VALUE_ROWS) * orthogonal(dir_b, gram_b)
    rows_a = (weights_a.astype(F32) * (1.0 - RATE * DECAY) - RATE * update_a).astype(BF16)
    rows_b = (up_weight_before.astype(F32) * (1.0 - RATE * DECAY) - RATE * update_b).astype(BF16)
    weight_a, weight_b = spread_call(dp, rows_a, rows_b)
    return (weight_a, new_a, update_a, weight_b, new_b, update_b)


def solution(mesh):
    both = P(("dp", "mp"), None)
    grads = P("dp", None, "mp", None)
    weights = P(None, "mp", None)
    return jax.shard_map(
        functools.partial(local, mesh.shape["dp"], mesh.shape["mp"]),
        mesh=mesh,
        in_specs=(grads, both, both, grads, both, both),
        out_specs=(weights, both, both, weights, both, both),
        check_vma=False,
    )
```

```python
import functools
import math

import jax
import jax.numpy as jnp
from jax import lax
from jax.experimental import pallas as pl
from jax.experimental.pallas import tpu as pltpu
from jax.sharding import PartitionSpec as P

D = 7168
KEY_VALUE_ROWS = 16384
ITERS = 3

COEF_A = 3.4445
COEF_B = -4.775
COEF_C = 2.0315
MOMENT = 0.95
RATE = 0.2
DECAY = 0.1
EPSILON = 1e-07
MESH = pl.DeviceIdType.MESH
F32 = jnp.float32
BF16 = jnp.bfloat16
BLOCK = 128
TILE = 256


def padded(columns):
    return -(-columns // BLOCK) * BLOCK


def block_list(columns):
    count = padded(columns) // BLOCK
    return [(i, j) for i in range(count) for j in range(i, count)]


def packed_rows(columns, devices):
    unit = 8 * devices
    return -(-len(block_list(columns)) * BLOCK // unit) * unit


def split(value):
    high = value.astype(BF16)
    return high, (value - high.astype(F32)).astype(BF16)


def greet(others):
    barrier = pltpu.get_barrier_semaphore()
    for other in others:
        pl.semaphore_signal(barrier, inc=1, device_id=other, device_id_type=MESH)
    pl.semaphore_wait(barrier, len(others))


def remote(src, dst, send, recv, target):
    return pltpu.make_async_remote_copy(
        src_ref=src, dst_ref=dst, send_sem=send, recv_sem=recv, device_id=target, device_id_type=MESH
    )


def rows_at(start, size):
    return pl.ds(pl.multiple_of(start, 8), size)


class Side:
    def __init__(self, place, gain, grads, mom_in, old_in, out_weight, out_state, out_update, scratch):
        self.place, self.gain = place, gain
        self.grads, self.mom_in, self.old_in = grads, mom_in, old_in
        self.out_weight, self.out_state, self.out_update = out_weight, out_state, out_update
        (
            self.own, self.got, self.mom, self.old, self.state, self.update, self.rows, self.iterate,
            self.pack, self.half, self.quarter, self.part, self.red, self.quart_recv, self.part_recv,
            self.gram, self.poly, self.inner, self.left, self.right,
            self.in_sem, self.out_sem, self.rs_send, self.rs_recv, self.core_sem,
            self.dp_sem, self.line_sem, self.ag_send, self.ag_recv,
        ) = scratch
        self.d, self.m, self.core, self.sibling, self.group, self.line = place
        self.columns = self.mom.shape[1]
        self.wide = self.iterate.shape[1]
        self.z = self.m // 2
        self.total = self.pack.shape[0]
        self.half_rows = self.total // 2
        self.quarter_rows = self.quarter.shape[0]
        self.part_rows = self.part.shape[0]
        self.my_half = self.core * self.half_rows
        self.my_quarter = self.my_half + self.d * self.quarter_rows
        self.my_part = self.my_quarter + self.z * self.part_rows
        self.sent = []

    def load(self):
        self.loads = []
        for i, (src, dst) in enumerate(
            ((self.grads.at[0, self.d], self.own), (self.mom_in, self.mom), (self.old_in, self.old))
        ):
            copy = pltpu.make_async_copy(src, dst, self.in_sem.at[i])
            copy.start()
            self.loads.append(copy)

    def scatter(self):
        self.scattered = []
        for r, target in enumerate(self.group):
            copy = remote(
                self.grads.at[0, target[0]], self.got.at[r], self.rs_send.at[r], self.rs_recv.at[r], target
            )
            copy.start()
            self.scattered.append(copy)

    def scatter_sent(self):
        for copy in self.scattered:
            copy.wait_send()

    def local_gram(self):
        used = len(block_list(self.columns)) * BLOCK
        if self.total > used:
            self.pack[used:, :] = jnp.zeros((self.total - used, BLOCK), F32)
        if self.wide > self.columns:
            self.iterate[...] = jnp.zeros(self.iterate.shape, F32)
        for ref in (self.gram, self.poly, self.inner):
            if self.wide > self.columns:
                ref[...] = jnp.zeros(ref.shape, F32)
        for copy in self.loads:
            copy.wait()
        for copy in self.scattered:
            copy.wait_recv()
        summed = self.own[...].astype(F32)
        for r in range(len(self.group)):
            summed = summed + self.got[r].astype(F32)
        state = MOMENT * self.mom[...] + summed
        self.state[...] = state
        self.iterate[:, : self.columns] = summed + MOMENT * state
        self.outs = [pltpu.make_async_copy(self.state, self.out_state, self.out_sem.at[0])]
        self.outs[0].start()
        high, low = split(self.iterate[...])

        def product(x, y):
            return lax.dot_general(x, y, (((0,), (0,)), ((), ())), preferred_element_type=F32)

        at = 0
        count = self.wide // BLOCK
        for i in range(count):
            left, right = slice(i * BLOCK, (i + 1) * BLOCK), slice(i * BLOCK, count * BLOCK)
            row = (
                product(high[:, left], high[:, right])
                + product(high[:, left], low[:, right])
                + product(low[:, left], high[:, right])
            )
            for j in range(count - i):
                self.pack[at : at + BLOCK, :] = row[:, j * BLOCK : (j + 1) * BLOCK]
                at += BLOCK

    def start(self, copies):
        self.flying = copies
        for copy in copies:
            copy.start()

    def arrived(self):
        for copy in self.flying:
            copy.wait_recv()
        self.sent += self.flying

    def core_start(self):
        src = self.pack.at[rows_at((1 - self.core) * self.half_rows, self.half_rows)]
        self.start([remote(src, self.half, self.core_sem.at[0], self.core_sem.at[1], self.sibling)])

    def core_end(self):
        self.arrived()
        self.half[...] = self.half[...] + self.pack[rows_at(self.my_half, self.half_rows), :]

    def dp_start(self):
        self.start([
            remote(
                self.half.at[rows_at(target[0] * self.quarter_rows, self.quarter_rows)], self.quart_recv.at[r],
                self.dp_sem.at[0, r], self.dp_sem.at[1, r], target,
            )
            for r, target in enumerate(self.group)
        ])

    def dp_end(self):
        self.arrived()
        value = self.half[rows_at(self.d * self.quarter_rows, self.quarter_rows), :]
        for r in range(len(self.group)):
            value = value + self.quart_recv[r]
        self.quarter[...] = value

    def line_start(self):
        self.start([
            remote(
                self.quarter.at[rows_at((target[1] // 2) * self.part_rows, self.part_rows)], self.part_recv.at[r],
                self.line_sem.at[0, r], self.line_sem.at[1, r], target,
            )
            for r, target in enumerate(self.line)
        ])

    def line_end(self):
        self.arrived()
        value = self.quarter[rows_at(self.z * self.part_rows, self.part_rows), :]
        for r in range(len(self.line)):
            value = value + self.part_recv[r]
        self.red[rows_at(self.my_part, self.part_rows), :] = value

    def line_back(self):
        spot = self.red.at[rows_at(self.my_part, self.part_rows)]
        self.start([
            remote(spot, spot, self.line_sem.at[2, r], self.line_sem.at[3, r], target)
            for r, target in enumerate(self.line)
        ])

    def dp_back(self):
        spot = self.red.at[rows_at(self.my_quarter, self.quarter_rows)]
        self.start([
            remote(spot, spot, self.dp_sem.at[2, r], self.dp_sem.at[3, r], target)
            for r, target in enumerate(self.group)
        ])

    def core_back(self):
        spot = self.red.at[rows_at(self.my_half, self.half_rows)]
        self.start([remote(spot, spot, self.core_sem.at[2], self.core_sem.at[3], self.sibling)])

    def unpack(self):
        trace = jnp.zeros((1, 1), F32)
        diagonal = lax.broadcasted_iota(jnp.int32, (BLOCK, BLOCK), 0) == lax.broadcasted_iota(
            jnp.int32, (BLOCK, BLOCK), 1
        )
        for k, (i, j) in enumerate(block_list(self.columns)):
            if i == j:
                block = self.red[k * BLOCK : (k + 1) * BLOCK, :]
                trace = trace + jnp.sum(jnp.where(diagonal, block, 0.0), keepdims=True)
        scale = 1.0 / (jnp.sqrt(trace) + EPSILON)
        for k, (i, j) in enumerate(block_list(self.columns)):
            block = self.red[k * BLOCK : (k + 1) * BLOCK, :] * scale * scale
            up, down = slice(i * BLOCK, (i + 1) * BLOCK), slice(j * BLOCK, (j + 1) * BLOCK)
            self.gram[up, down] = block
            if i != j:
                self.gram[down, up] = block.T
        self.iterate[...] = self.iterate[...] * scale

    def set_left(self, value):
        high, low = split(value)
        self.left[:, : self.wide] = high
        self.left[:, self.wide : 2 * self.wide] = high
        self.left[:, 2 * self.wide :] = low

    def set_right(self, value):
        high, low = split(value)
        self.right[: self.wide, :] = high
        self.right[self.wide : 2 * self.wide, :] = low
        self.right[2 * self.wide :, :] = high

    def product(self, out, coefficient, base, base_coefficient):
        for at in range(0, self.wide, TILE):
            to = min(at + TILE, self.wide)
            cols = slice(at, to)
            value = jnp.dot(
                self.left[at : self.columns, :], self.right[:, cols], preferred_element_type=F32
            )
            out[at : self.columns, cols] = (
                base_coefficient * base[at : self.columns, cols] + coefficient * value
            )
            if to < self.wide:
                out[cols, to:] = out[to:, cols].T

    def newton(self, step):
        gram = self.gram[...]
        self.set_left(gram)
        self.set_right(gram)
        self.product(self.poly, COEF_C, self.gram, COEF_B)
        self.set_right(self.poly[...])
        value = self.iterate[...]
        high, low = split(value)
        self.iterate[...] = COEF_A * value + jnp.dot(
            jnp.concatenate([high, high, low], axis=1), self.right[...], preferred_element_type=F32
        )
        if step < ITERS - 1:
            self.product(self.inner, 1.0, self.gram, COEF_A)
            self.set_left(self.poly[...])
            self.set_right(self.inner[...])
            self.product(self.gram, 1.0, self.inner, COEF_A)

    def finish(self):
        update = self.gain * self.iterate[:, : self.columns]
        self.rows[...] = (self.old[...].astype(F32) * (1.0 - RATE * DECAY) - RATE * update).astype(BF16)
        self.update[...] = update

    def spread(self, near, far):
        self.first = []
        for side, target in enumerate((near, far)):
            copy = remote(
                self.rows, self.out_weight.at[self.d], self.ag_send.at[side], self.ag_recv.at[side], target
            )
            copy.start()
            self.first.append(copy)
        for i, (src, dst) in enumerate(
            ((self.rows, self.out_weight.at[self.d]), (self.update, self.out_update))
        ):
            copy = pltpu.make_async_copy(src, dst, self.out_sem.at[1 + i])
            copy.start()
            self.outs.append(copy)

    def forward(self, near, far):
        count = self.rows.shape[0]
        cut = count // 2 // 16 * 16
        self.later = []
        for side, (source, target, start, size) in enumerate(
            ((near[0], far, 0, cut), (far[0], near, cut, count - cut))
        ):
            self.first[side].wait_recv()
            if size:
                out = self.out_weight
                spot = out.at[source] if size == count else out.at[source, pl.ds(start, size)]
                copy = remote(spot, spot, self.ag_send.at[2 + side], self.ag_recv.at[2 + side], target)
                copy.start()
                self.later.append(copy)

    def end(self):
        for copy in self.outs + self.later:
            copy.wait()
        for copy in self.first + self.sent:
            copy.wait_send()


def kernel(dp, mp, *refs):
    d, m = lax.axis_index("dp"), lax.axis_index("mp")
    core = lax.rem(m, 2)
    sibling = (d, m + 1 - 2 * core)
    group = [(lax.rem(d + r, dp), m) for r in range(1, dp)]
    line = [(d, lax.rem(m + 2 * r, mp)) for r in range(1, mp // 2)]
    near = (d + 1 - 2 * lax.rem(d, 2), m)
    far = (lax.rem(d + 2, dp), m)
    place = (d, m, core, sibling, group, line)
    scratch = refs[12:]
    count = len(scratch) // 2
    a = Side(place, 0.2 * math.sqrt(D), *refs[0:3], *refs[6:9], scratch[:count])
    b = Side(place, 0.2 * math.sqrt(KEY_VALUE_ROWS), *refs[3:6], *refs[9:12], scratch[count:])
    b.load()
    a.load()
    greet([sibling] + group + line)
    b.scatter()
    b.scatter_sent()
    a.scatter()
    b.local_gram()
    b.core_start()
    b.core_end()
    b.dp_start()
    a.local_gram()
    a.core_start()
    b.dp_end()
    b.line_start()
    a.core_end()
    a.dp_start()
    b.line_end()
    b.line_back()
    a.dp_end()
    a.line_start()
    b.arrived()
    b.dp_back()
    a.line_end()
    a.line_back()
    b.arrived()
    b.core_back()
    a.arrived()
    a.dp_back()
    b.arrived()
    b.unpack()
    b.newton(0)
    a.arrived()
    a.core_back()
    for step in range(1, ITERS):
        b.newton(step)
    b.finish()
    b.spread(near, far)
    a.arrived()
    a.unpack()
    for step in range(ITERS):
        a.newton(step)
    a.finish()
    a.spread(near, far)
    b.forward(near, far)
    a.forward(near, far)
    a.scatter_sent()
    a.end()
    b.end()


def scratch_of(dp, mp, rows, columns):
    zn = mp // 2
    wide = padded(columns)
    total = packed_rows(columns, dp * mp)
    half = total // 2
    quarter = half // dp
    part = quarter // zn
    vmem, sem = pltpu.VMEM, pltpu.SemaphoreType.DMA
    return [
        vmem((rows, columns), BF16),
        vmem((dp - 1, rows, columns), BF16),
        vmem((rows, columns), F32),
        vmem((rows, columns), BF16),
        vmem((rows, columns), F32),
        vmem((rows, columns), F32),
        vmem((rows, columns), BF16),
        vmem((rows, wide), F32),
        vmem((total, BLOCK), F32),
        vmem((half, BLOCK), F32),
        vmem((quarter, BLOCK), F32),
        vmem((part, BLOCK), F32),
        vmem((total, BLOCK), F32),
        vmem((dp - 1, quarter, BLOCK), F32),
        vmem((zn - 1, part, BLOCK), F32),
        vmem((wide, wide), F32),
        vmem((wide, wide), F32),
        vmem((wide, wide), F32),
        vmem((wide, 3 * wide), BF16),
        vmem((3 * wide, wide), BF16),
        sem((3,)),
        sem((3,)),
        sem((dp - 1,)),
        sem((dp - 1,)),
        sem((4,)),
        sem((4, dp - 1)),
        sem((4, zn - 1)),
        sem((4,)),
        sem((4,)),
    ]


def local(dp, mp, *args):
    (ra, ca), (rb, cb) = args[1].shape, args[4].shape
    hbm = pl.BlockSpec(memory_space=pl.ANY)
    shape = jax.ShapeDtypeStruct
    return pl.pallas_call(
        functools.partial(kernel, dp, mp),
        out_shape=[
            shape((dp, ra, ca), BF16), shape((ra, ca), F32), shape((ra, ca), F32),
            shape((dp, rb, cb), BF16), shape((rb, cb), F32), shape((rb, cb), F32),
        ],
        in_specs=[hbm] * 6,
        out_specs=[hbm] * 6,
        scratch_shapes=scratch_of(dp, mp, ra, ca) + scratch_of(dp, mp, rb, cb),
        compiler_params=pltpu.CompilerParams(
            collective_id=0, has_side_effects=True, vmem_limit_bytes=56 * 2**20
        ),
    )(*args)


def solution(mesh):
    both = P(("dp", "mp"), None)
    grads = P("dp", None, "mp", None)
    weights = P(None, "mp", None)
    return jax.shard_map(
        functools.partial(local, mesh.shape["dp"], mesh.shape["mp"]),
        mesh=mesh,
        in_specs=(grads, both, both, grads, both, both),
        out_specs=(weights, both, both, weights, both, both),
        check_vma=False,
    )
```

```python
import functools
import math

import jax
import jax.numpy as jnp
from jax import lax
from jax.experimental import pallas as pl
from jax.experimental.pallas import tpu as pltpu
from jax.sharding import PartitionSpec as P

D = 7168
KEY_VALUE_ROWS = 16384
ITERS = 3

COEF_A = 3.4445
COEF_B = -4.775
COEF_C = 2.0315
MOMENT = 0.95
RATE = 0.2
DECAY = 0.1
EPSILON = 1e-07
MESH = pl.DeviceIdType.MESH
F32 = jnp.float32
BF16 = jnp.bfloat16
BLOCK = 128
TILE = 256


def padded(columns):
    return -(-columns // BLOCK) * BLOCK


def block_list(columns):
    count = padded(columns) // BLOCK
    return [(i, j) for i in range(count) for j in range(i, count)]


def packed_rows(columns, devices):
    unit = 8 * devices
    return -(-len(block_list(columns)) * BLOCK // unit) * unit


def split(value):
    high = value.astype(BF16)
    return high, (value - high.astype(F32)).astype(BF16)


def greet(others):
    barrier = pltpu.get_barrier_semaphore()
    for other in others:
        pl.semaphore_signal(barrier, inc=1, device_id=other, device_id_type=MESH)
    pl.semaphore_wait(barrier, len(others))


def remote(src, dst, send, recv, target):
    return pltpu.make_async_remote_copy(
        src_ref=src, dst_ref=dst, send_sem=send, recv_sem=recv, device_id=target, device_id_type=MESH
    )


def rows_at(start, size):
    return pl.ds(pl.multiple_of(start, 8), size)


def part_of(ref, start, size):
    return ref if size == ref.shape[-2] else ref.at[pl.ds(start, size)]


class Side:
    def __init__(self, place, gain, grads, mom_in, old_in, out_weight, out_state, out_update, scratch):
        self.place, self.gain = place, gain
        self.grads, self.mom_in, self.old_in = grads, mom_in, old_in
        self.out_weight, self.out_state, self.out_update = out_weight, out_state, out_update
        (
            self.own, self.pair_own, self.pair_got, self.pair_sum, self.last_got, self.mom, self.old, self.state, self.update, self.rows, self.iterate,
            self.pack, self.half, self.quarter, self.part, self.red, self.quart_recv, self.part_recv,
            self.gram, self.poly, self.inner, self.left, self.right,
            self.in_sem, self.out_sem, self.rs_send, self.rs_recv, self.core_sem,
            self.dp_sem, self.line_sem, self.ag_send, self.ag_recv,
        ) = scratch
        self.d, self.m, self.core, self.sibling, self.group, self.line, near, far, across = place
        self.columns = self.mom.shape[1]
        self.wide = self.iterate.shape[1]
        self.z = self.m // 2
        self.total = self.pack.shape[0]
        self.half_rows = self.total // 2
        self.quarter_rows = self.quarter.shape[0]
        self.part_rows = self.part.shape[0]
        self.my_half = self.core * self.half_rows
        self.my_quarter = self.my_half + self.d * self.quarter_rows
        self.my_part = self.my_quarter + self.z * self.part_rows
        self.sent = []
        count = self.own.shape[0]
        cut = count // 2 // 16 * 16
        self.ways = [
            (way, start, size, first, second)
            for way, (start, size, first, second) in enumerate(
                ((0, cut, near, far), (cut, count - cut, far, near))
            )
            if size
        ]
        self.across = across

    def load(self):
        self.loads = []
        pairs = [(self.grads.at[0, self.d], self.own), (self.mom_in, self.mom), (self.old_in, self.old)]
        for way, start, size, first, second in self.ways:
            pairs.append(
                (part_of(self.grads.at[0, second[0]], start, size), part_of(self.pair_own, start, size))
            )
        for i, (src, dst) in enumerate(pairs):
            copy = pltpu.make_async_copy(src, dst, self.in_sem.at[i])
            copy.start()
            self.loads.append(copy)

    def scatter(self):
        self.scattered = {}
        for kind in range(2):
            for way, start, size, first, second in self.ways:
                owner = self.across if kind == 0 else first[0]
                copy = remote(
                    part_of(self.grads.at[0, owner], start, size), part_of(self.pair_got.at[kind], start, size),
                    self.rs_send.at[kind, way], self.rs_recv.at[kind, way], first,
                )
                copy.start()
                self.scattered[kind, way] = copy

    def scatter_sent(self):
        for copy in self.scattered.values():
            copy.wait_send()

    def scatter_pairs(self):
        for i in range(len(self.ways)):
            self.loads[3 + i].wait()
        for way, start, size, first, second in self.ways:
            self.scattered[0, way].wait_recv()
            rows = slice(start, start + size)
            self.pair_sum[rows] = (
                self.pair_own[rows].astype(F32) + self.pair_got[0, rows].astype(F32)
            ).astype(BF16)
            copy = remote(
                part_of(self.pair_sum, start, size), part_of(self.last_got, start, size),
                self.rs_send.at[2, way], self.rs_recv.at[2, way], second,
            )
            copy.start()
            self.scattered[2, way] = copy

    def local_gram(self):
        used = len(block_list(self.columns)) * BLOCK
        if self.total > used:
            self.pack[used:, :] = jnp.zeros((self.total - used, BLOCK), F32)
        if self.wide > self.columns:
            self.iterate[...] = jnp.zeros(self.iterate.shape, F32)
        for ref in (self.gram, self.poly, self.inner):
            if self.wide > self.columns:
                ref[...] = jnp.zeros(ref.shape, F32)
        for copy in self.loads[:3]:
            copy.wait()
        for kind in (1, 2):
            for way, *_ in self.ways:
                self.scattered[kind, way].wait_recv()
        summed = (
            self.own[...].astype(F32) + self.pair_got[1].astype(F32) + self.last_got[...].astype(F32)
        )
        state = MOMENT * self.mom[...] + summed
        self.state[...] = state
        self.iterate[:, : self.columns] = summed + MOMENT * state
        self.outs = [pltpu.make_async_copy(self.state, self.out_state, self.out_sem.at[0])]
        self.outs[0].start()
        high, low = split(self.iterate[...])

        def product(x, y):
            return lax.dot_general(x, y, (((0,), (0,)), ((), ())), preferred_element_type=F32)

        at = 0
        count = self.wide // BLOCK
        for i in range(count):
            left, right = slice(i * BLOCK, (i + 1) * BLOCK), slice(i * BLOCK, count * BLOCK)
            row = (
                product(high[:, left], high[:, right])
                + product(high[:, left], low[:, right])
                + product(low[:, left], high[:, right])
            )
            for j in range(count - i):
                self.pack[at : at + BLOCK, :] = row[:, j * BLOCK : (j + 1) * BLOCK]
                at += BLOCK

    def start(self, copies):
        self.flying = copies
        for copy in copies:
            copy.start()

    def arrived(self):
        for copy in self.flying:
            copy.wait_recv()
        self.sent += self.flying

    def core_start(self):
        src = self.pack.at[rows_at((1 - self.core) * self.half_rows, self.half_rows)]
        self.start([remote(src, self.half, self.core_sem.at[0], self.core_sem.at[1], self.sibling)])

    def core_end(self):
        self.arrived()
        self.half[...] = self.half[...] + self.pack[rows_at(self.my_half, self.half_rows), :]

    def dp_start(self):
        self.start([
            remote(
                self.half.at[rows_at(target[0] * self.quarter_rows, self.quarter_rows)], self.quart_recv.at[r],
                self.dp_sem.at[0, r], self.dp_sem.at[1, r], target,
            )
            for r, target in enumerate(self.group)
        ])

    def dp_end(self):
        self.arrived()
        value = self.half[rows_at(self.d * self.quarter_rows, self.quarter_rows), :]
        for r in range(len(self.group)):
            value = value + self.quart_recv[r]
        self.quarter[...] = value

    def line_start(self):
        self.start([
            remote(
                self.quarter.at[rows_at((target[1] // 2) * self.part_rows, self.part_rows)], self.part_recv.at[r],
                self.line_sem.at[0, r], self.line_sem.at[1, r], target,
            )
            for r, target in enumerate(self.line)
        ])

    def line_end(self):
        self.arrived()
        value = self.quarter[rows_at(self.z * self.part_rows, self.part_rows), :]
        for r in range(len(self.line)):
            value = value + self.part_recv[r]
        self.red[rows_at(self.my_part, self.part_rows), :] = value

    def line_back(self):
        spot = self.red.at[rows_at(self.my_part, self.part_rows)]
        self.start([
            remote(spot, spot, self.line_sem.at[2, r], self.line_sem.at[3, r], target)
            for r, target in enumerate(self.line)
        ])

    def dp_back(self):
        spot = self.red.at[rows_at(self.my_quarter, self.quarter_rows)]
        self.start([
            remote(spot, spot, self.dp_sem.at[2, r], self.dp_sem.at[3, r], target)
            for r, target in enumerate(self.group)
        ])

    def core_back(self):
        spot = self.red.at[rows_at(self.my_half, self.half_rows)]
        self.start([remote(spot, spot, self.core_sem.at[2], self.core_sem.at[3], self.sibling)])

    def unpack(self):
        trace = jnp.zeros((1, 1), F32)
        diagonal = lax.broadcasted_iota(jnp.int32, (BLOCK, BLOCK), 0) == lax.broadcasted_iota(
            jnp.int32, (BLOCK, BLOCK), 1
        )
        for k, (i, j) in enumerate(block_list(self.columns)):
            if i == j:
                block = self.red[k * BLOCK : (k + 1) * BLOCK, :]
                trace = trace + jnp.sum(jnp.where(diagonal, block, 0.0), keepdims=True)
        scale = 1.0 / (jnp.sqrt(trace) + EPSILON)
        for k, (i, j) in enumerate(block_list(self.columns)):
            block = self.red[k * BLOCK : (k + 1) * BLOCK, :] * scale * scale
            up, down = slice(i * BLOCK, (i + 1) * BLOCK), slice(j * BLOCK, (j + 1) * BLOCK)
            self.gram[up, down] = block
            if i != j:
                self.gram[down, up] = block.T
        self.iterate[...] = self.iterate[...] * scale

    def set_left(self, value):
        high, low = split(value)
        self.left[:, : self.wide] = high
        self.left[:, self.wide : 2 * self.wide] = high
        self.left[:, 2 * self.wide :] = low

    def set_right(self, value):
        high, low = split(value)
        self.right[: self.wide, :] = high
        self.right[self.wide : 2 * self.wide, :] = low
        self.right[2 * self.wide :, :] = high

    def product(self, out, coefficient, base, base_coefficient):
        for at in range(0, self.wide, TILE):
            to = min(at + TILE, self.wide)
            cols = slice(at, to)
            value = jnp.dot(
                self.left[at : self.columns, :], self.right[:, cols], preferred_element_type=F32
            )
            out[at : self.columns, cols] = (
                base_coefficient * base[at : self.columns, cols] + coefficient * value
            )
            if to < self.wide:
                out[cols, to:] = out[to:, cols].T

    def newton(self, step):
        gram = self.gram[...]
        self.set_left(gram)
        self.set_right(gram)
        self.product(self.poly, COEF_C, self.gram, COEF_B)
        self.set_right(self.poly[...])
        value = self.iterate[...]
        high, low = split(value)
        self.iterate[...] = COEF_A * value + jnp.dot(
            jnp.concatenate([high, high, low], axis=1), self.right[...], preferred_element_type=F32
        )
        if step < ITERS - 1:
            self.product(self.inner, 1.0, self.gram, COEF_A)
            self.set_left(self.poly[...])
            self.set_right(self.inner[...])
            self.product(self.gram, 1.0, self.inner, COEF_A)

    def finish(self):
        update = self.gain * self.iterate[:, : self.columns]
        self.rows[...] = (self.old[...].astype(F32) * (1.0 - RATE * DECAY) - RATE * update).astype(BF16)
        self.update[...] = update

    def spread(self, near, far):
        self.first = []
        for side, target in enumerate((near, far)):
            copy = remote(
                self.rows, self.out_weight.at[self.d], self.ag_send.at[side], self.ag_recv.at[side], target
            )
            copy.start()
            self.first.append(copy)
        for i, (src, dst) in enumerate(
            ((self.rows, self.out_weight.at[self.d]), (self.update, self.out_update))
        ):
            copy = pltpu.make_async_copy(src, dst, self.out_sem.at[1 + i])
            copy.start()
            self.outs.append(copy)

    def forward(self, near, far):
        count = self.rows.shape[0]
        cut = count // 2 // 16 * 16
        self.later = []
        for side, (source, target, start, size) in enumerate(
            ((near[0], far, 0, cut), (far[0], near, cut, count - cut))
        ):
            self.first[side].wait_recv()
            if size:
                out = self.out_weight
                spot = out.at[source] if size == count else out.at[source, pl.ds(start, size)]
                copy = remote(spot, spot, self.ag_send.at[2 + side], self.ag_recv.at[2 + side], target)
                copy.start()
                self.later.append(copy)

    def end(self):
        for copy in self.outs + self.later:
            copy.wait()
        for copy in self.first + self.sent:
            copy.wait_send()


def kernel(dp, mp, *refs):
    d, m = lax.axis_index("dp"), lax.axis_index("mp")
    core = lax.rem(m, 2)
    sibling = (d, m + 1 - 2 * core)
    group = [(lax.rem(d + r, dp), m) for r in range(1, dp)]
    line = [(d, lax.rem(m + 2 * r, mp)) for r in range(1, mp // 2)]
    near = (d + 1 - 2 * lax.rem(d, 2), m)
    far = (lax.rem(d + 2, dp), m)
    across = near[0] + 2 - 4 * (d // 2)
    place = (d, m, core, sibling, group, line, near, far, across)
    scratch = refs[12:]
    count = len(scratch) // 2
    a = Side(place, 0.2 * math.sqrt(D), *refs[0:3], *refs[6:9], scratch[:count])
    b = Side(place, 0.2 * math.sqrt(KEY_VALUE_ROWS), *refs[3:6], *refs[9:12], scratch[count:])
    b.load()
    a.load()
    greet([sibling] + group + line)
    b.scatter()
    b.scatter_sent()
    a.scatter()
    b.scatter_pairs()
    a.scatter_sent()
    a.scatter_pairs()
    b.local_gram()
    b.core_start()
    b.core_end()
    b.dp_start()
    a.local_gram()
    a.core_start()
    b.dp_end()
    b.line_start()
    a.core_end()
    a.dp_start()
    b.line_end()
    b.line_back()
    a.dp_end()
    a.line_start()
    b.arrived()
    b.dp_back()
    a.line_end()
    a.line_back()
    b.arrived()
    b.core_back()
    a.arrived()
    a.dp_back()
    b.arrived()
    b.unpack()
    b.newton(0)
    a.arrived()
    a.core_back()
    for step in range(1, ITERS):
        b.newton(step)
    b.finish()
    b.spread(near, far)
    a.arrived()
    a.unpack()
    for step in range(ITERS):
        a.newton(step)
    a.finish()
    a.spread(near, far)
    b.forward(near, far)
    a.forward(near, far)
    for side in (a, b):
        for way, *_ in side.ways:
            side.scattered[2, way].wait_send()
    a.end()
    b.end()


def scratch_of(dp, mp, rows, columns):
    zn = mp // 2
    wide = padded(columns)
    total = packed_rows(columns, dp * mp)
    half = total // 2
    quarter = half // dp
    part = quarter // zn
    vmem, sem = pltpu.VMEM, pltpu.SemaphoreType.DMA
    return [
        vmem((rows, columns), BF16),
        vmem((rows, columns), BF16),
        vmem((2, rows, columns), BF16),
        vmem((rows, columns), BF16),
        vmem((rows, columns), BF16),
        vmem((rows, columns), F32),
        vmem((rows, columns), BF16),
        vmem((rows, columns), F32),
        vmem((rows, columns), F32),
        vmem((rows, columns), BF16),
        vmem((rows, wide), F32),
        vmem((total, BLOCK), F32),
        vmem((half, BLOCK), F32),
        vmem((quarter, BLOCK), F32),
        vmem((part, BLOCK), F32),
        vmem((total, BLOCK), F32),
        vmem((dp - 1, quarter, BLOCK), F32),
        vmem((zn - 1, part, BLOCK), F32),
        vmem((wide, wide), F32),
        vmem((wide, wide), F32),
        vmem((wide, wide), F32),
        vmem((wide, 3 * wide), BF16),
        vmem((3 * wide, wide), BF16),
        sem((5,)),
        sem((3,)),
        sem((3, 2)),
        sem((3, 2)),
        sem((4,)),
        sem((4, dp - 1)),
        sem((4, zn - 1)),
        sem((4,)),
        sem((4,)),
    ]


def local(dp, mp, *args):
    (ra, ca), (rb, cb) = args[1].shape, args[4].shape
    hbm = pl.BlockSpec(memory_space=pl.ANY)
    shape = jax.ShapeDtypeStruct
    results = pl.pallas_call(
        functools.partial(kernel, dp, mp),
        out_shape=[
            shape((dp, ra, ca), BF16), shape((ra, ca), F32), shape((ra, ca), F32),
            shape((dp, rb, cb), BF16), shape((rb, cb), F32), shape((rb, cb), F32),
        ],
        in_specs=[hbm] * 6,
        out_specs=[hbm] * 6,
        scratch_shapes=scratch_of(dp, mp, ra, ca) + scratch_of(dp, mp, rb, cb),
        compiler_params=pltpu.CompilerParams(
            collective_id=0, has_side_effects=True, vmem_limit_bytes=56 * 2**20
        ),
    )(*args)
    return place_results(results)


def place_kernel(count, *refs):
    sem = refs[-1]
    copies = []
    for src, dst in zip(refs[:count], refs[count : 2 * count]):
        rows = src.shape[-2]
        if len(src.shape) == 3:
            views = [(k,) for k in range(src.shape[0])]
        else:
            pieces = 4 if rows % 64 == 0 else 2 if rows % 32 == 0 else 1
            size = rows // pieces
            views = [(pl.ds(k * size, size),) for k in range(pieces)]
        for view in views:
            copies.append(pltpu.make_async_copy(src.at[view], dst.at[view], sem.at[len(copies)]))
    for copy in copies:
        copy.start()
    for copy in copies:
        copy.wait()


def place_results(results):
    count = len(results)
    hbm = pl.BlockSpec(memory_space=pl.ANY)
    return pl.pallas_call(
        functools.partial(place_kernel, count),
        out_shape=[jax.ShapeDtypeStruct(r.shape, r.dtype) for r in results],
        in_specs=[hbm] * count,
        out_specs=[hbm] * count,
        scratch_shapes=[pltpu.SemaphoreType.DMA((4 * count,))],
        compiler_params=pltpu.CompilerParams(vmem_limit_bytes=56 * 2**20),
    )(*results)


def solution(mesh):
    both = P(("dp", "mp"), None)
    grads = P("dp", None, "mp", None)
    weights = P(None, "mp", None)
    return jax.shard_map(
        functools.partial(local, mesh.shape["dp"], mesh.shape["mp"]),
        mesh=mesh,
        in_specs=(grads, both, both, grads, both, both),
        out_specs=(weights, both, both, weights, both, both),
        check_vma=False,
    )
```

```python
import functools
import math

import jax
import jax.numpy as jnp
from jax import lax
from jax.experimental import pallas as pl
from jax.experimental.pallas import tpu as pltpu
from jax.sharding import PartitionSpec as P

D = 7168
KEY_VALUE_ROWS = 16384
ITERS = 3

COEF_A = 3.4445
COEF_B = -4.775
COEF_C = 2.0315
MOMENT = 0.95
RATE = 0.2
DECAY = 0.1
EPSILON = 1e-07
MESH = pl.DeviceIdType.MESH
F32 = jnp.float32
BF16 = jnp.bfloat16
BLOCK = 128
TILE = 256


def padded(columns):
    return -(-columns // BLOCK) * BLOCK


def block_list(columns):
    count = padded(columns) // BLOCK
    return [(i, j) for i in range(count) for j in range(i, count)]


def packed_rows(columns, devices):
    unit = 8 * devices
    return -(-len(block_list(columns)) * BLOCK // unit) * unit


def split(value):
    high = value.astype(BF16)
    return high, (value - high.astype(F32)).astype(BF16)


def greet(others):
    barrier = pltpu.get_barrier_semaphore()
    for other in others:
        pl.semaphore_signal(barrier, inc=1, device_id=other, device_id_type=MESH)
    pl.semaphore_wait(barrier, len(others))


def remote(src, dst, send, recv, target):
    return pltpu.make_async_remote_copy(
        src_ref=src, dst_ref=dst, send_sem=send, recv_sem=recv, device_id=target, device_id_type=MESH
    )


def rows_at(start, size):
    return pl.ds(pl.multiple_of(start, 8), size)


def part_of(ref, start, size):
    return ref if size == ref.shape[-2] else ref.at[pl.ds(start, size)]


class Side:
    def __init__(self, place, gain, grads, mom_in, old_in, out_weight, out_state, out_update, scratch):
        self.place, self.gain = place, gain
        self.grads, self.mom_in, self.old_in = grads, mom_in, old_in
        self.out_weight, self.out_state, self.out_update = out_weight, out_state, out_update
        (
            self.own, self.pair_own, self.pair_got, self.pair_sum, self.last_got, self.mom, self.old, self.state, self.update, self.rows, self.iterate,
            self.pack, self.half, self.quarter, self.part, self.red, self.quart_recv, self.part_recv,
            self.gram, self.poly, self.inner, self.left, self.right,
            self.in_sem, self.out_sem, self.rs_send, self.rs_recv, self.core_sem,
            self.dp_sem, self.line_sem, self.ag_send, self.ag_recv,
        ) = scratch
        self.d, self.m, self.core, self.sibling, self.group, self.line, near, far, across = place
        self.columns = self.mom.shape[1]
        self.wide = self.iterate.shape[1]
        self.z = self.m // 2
        self.total = self.pack.shape[0]
        self.half_rows = self.total // 2
        self.quarter_rows = self.quarter.shape[0]
        self.part_rows = self.part.shape[0]
        self.my_half = self.core * self.half_rows
        self.my_quarter = self.my_half + self.d * self.quarter_rows
        self.my_part = self.my_quarter + self.z * self.part_rows
        self.sent = []
        count = self.own.shape[0]
        cut = count // 2 // 16 * 16
        self.ways = [
            (way, start, size, first, second)
            for way, (start, size, first, second) in enumerate(
                ((0, cut, near, far), (cut, count - cut, far, near))
            )
            if size
        ]
        self.across = across

    def load(self):
        self.loads = []
        pairs = [(self.grads.at[0, self.d], self.own), (self.mom_in, self.mom), (self.old_in, self.old)]
        for way, start, size, first, second in self.ways:
            pairs.append(
                (part_of(self.grads.at[0, second[0]], start, size), part_of(self.pair_own, start, size))
            )
        for i, (src, dst) in enumerate(pairs):
            copy = pltpu.make_async_copy(src, dst, self.in_sem.at[i])
            copy.start()
            self.loads.append(copy)

    def scatter(self):
        self.scattered = {}
        for kind in range(2):
            for way, start, size, first, second in self.ways:
                owner = self.across if kind == 0 else first[0]
                copy = remote(
                    part_of(self.grads.at[0, owner], start, size), part_of(self.pair_got.at[kind], start, size),
                    self.rs_send.at[kind, way], self.rs_recv.at[kind, way], first,
                )
                copy.start()
                self.scattered[kind, way] = copy

    def scatter_sent(self):
        for copy in self.scattered.values():
            copy.wait_send()

    def scatter_pairs(self):
        for i in range(len(self.ways)):
            self.loads[3 + i].wait()
        for way, start, size, first, second in self.ways:
            self.scattered[0, way].wait_recv()
            rows = slice(start, start + size)
            self.pair_sum[rows] = (
                self.pair_own[rows].astype(F32) + self.pair_got[0, rows].astype(F32)
            ).astype(BF16)
            copy = remote(
                part_of(self.pair_sum, start, size), part_of(self.last_got, start, size),
                self.rs_send.at[2, way], self.rs_recv.at[2, way], second,
            )
            copy.start()
            self.scattered[2, way] = copy

    def local_gram(self):
        used = len(block_list(self.columns)) * BLOCK
        if self.total > used:
            self.pack[used:, :] = jnp.zeros((self.total - used, BLOCK), F32)
        if self.wide > self.columns:
            self.iterate[...] = jnp.zeros(self.iterate.shape, F32)
        for ref in (self.gram, self.poly, self.inner):
            if self.wide > self.columns:
                ref[...] = jnp.zeros(ref.shape, F32)
        for copy in self.loads[:3]:
            copy.wait()
        for kind in (1, 2):
            for way, *_ in self.ways:
                self.scattered[kind, way].wait_recv()
        summed = (
            self.own[...].astype(F32) + self.pair_got[1].astype(F32) + self.last_got[...].astype(F32)
        )
        state = MOMENT * self.mom[...] + summed
        self.state[...] = state
        self.iterate[:, : self.columns] = summed + MOMENT * state
        self.outs = [pltpu.make_async_copy(self.state, self.out_state, self.out_sem.at[0])]
        self.outs[0].start()
        high, low = split(self.iterate[...])

        def product(x, y):
            return lax.dot_general(x, y, (((0,), (0,)), ((), ())), preferred_element_type=F32)

        at = 0
        count = self.wide // BLOCK
        for i in range(count):
            left, right = slice(i * BLOCK, (i + 1) * BLOCK), slice(i * BLOCK, count * BLOCK)
            row = (
                product(high[:, left], high[:, right])
                + product(high[:, left], low[:, right])
                + product(low[:, left], high[:, right])
            )
            for j in range(count - i):
                self.pack[at : at + BLOCK, :] = row[:, j * BLOCK : (j + 1) * BLOCK]
                at += BLOCK

    def start(self, copies):
        self.flying = copies
        for copy in copies:
            copy.start()

    def arrived(self):
        for copy in self.flying:
            copy.wait_recv()
        self.sent += self.flying

    def core_start(self):
        src = self.pack.at[rows_at((1 - self.core) * self.half_rows, self.half_rows)]
        self.start([remote(src, self.half, self.core_sem.at[0], self.core_sem.at[1], self.sibling)])

    def core_end(self):
        self.arrived()
        self.half[...] = self.half[...] + self.pack[rows_at(self.my_half, self.half_rows), :]

    def dp_start(self):
        self.start([
            remote(
                self.half.at[rows_at(target[0] * self.quarter_rows, self.quarter_rows)], self.quart_recv.at[r],
                self.dp_sem.at[0, r], self.dp_sem.at[1, r], target,
            )
            for r, target in enumerate(self.group)
        ])

    def dp_end(self):
        self.arrived()
        value = self.half[rows_at(self.d * self.quarter_rows, self.quarter_rows), :]
        for r in range(len(self.group)):
            value = value + self.quart_recv[r]
        self.quarter[...] = value

    def line_start(self):
        self.start([
            remote(
                self.quarter.at[rows_at((target[1] // 2) * self.part_rows, self.part_rows)], self.part_recv.at[r],
                self.line_sem.at[0, r], self.line_sem.at[1, r], target,
            )
            for r, target in enumerate(self.line)
        ])

    def line_end(self):
        self.arrived()
        value = self.quarter[rows_at(self.z * self.part_rows, self.part_rows), :]
        for r in range(len(self.line)):
            value = value + self.part_recv[r]
        self.red[rows_at(self.my_part, self.part_rows), :] = value

    def line_back(self):
        spot = self.red.at[rows_at(self.my_part, self.part_rows)]
        self.start([
            remote(spot, spot, self.line_sem.at[2, r], self.line_sem.at[3, r], target)
            for r, target in enumerate(self.line)
        ])

    def dp_back(self):
        spot = self.red.at[rows_at(self.my_quarter, self.quarter_rows)]
        self.start([
            remote(spot, spot, self.dp_sem.at[2, r], self.dp_sem.at[3, r], target)
            for r, target in enumerate(self.group)
        ])

    def core_back(self):
        spot = self.red.at[rows_at(self.my_half, self.half_rows)]
        self.start([remote(spot, spot, self.core_sem.at[2], self.core_sem.at[3], self.sibling)])

    def unpack(self):
        trace = jnp.zeros((1, 1), F32)
        diagonal = lax.broadcasted_iota(jnp.int32, (BLOCK, BLOCK), 0) == lax.broadcasted_iota(
            jnp.int32, (BLOCK, BLOCK), 1
        )
        for k, (i, j) in enumerate(block_list(self.columns)):
            if i == j:
                block = self.red[k * BLOCK : (k + 1) * BLOCK, :]
                trace = trace + jnp.sum(jnp.where(diagonal, block, 0.0), keepdims=True)
        scale = 1.0 / (jnp.sqrt(trace) + EPSILON)
        for k, (i, j) in enumerate(block_list(self.columns)):
            block = self.red[k * BLOCK : (k + 1) * BLOCK, :] * scale * scale
            up, down = slice(i * BLOCK, (i + 1) * BLOCK), slice(j * BLOCK, (j + 1) * BLOCK)
            self.gram[up, down] = block
            if i != j:
                self.gram[down, up] = block.T
        self.iterate[...] = self.iterate[...] * scale

    def set_left(self, value):
        high, low = split(value)
        self.left[:, : self.wide] = high
        self.left[:, self.wide : 2 * self.wide] = high
        self.left[:, 2 * self.wide :] = low

    def set_right(self, value):
        high, low = split(value)
        self.right[: self.wide, :] = high
        self.right[self.wide : 2 * self.wide, :] = low
        self.right[2 * self.wide :, :] = high

    def product(self, out, coefficient, base, base_coefficient):
        for at in range(0, self.wide, TILE):
            to = min(at + TILE, self.wide)
            cols = slice(at, to)
            value = jnp.dot(
                self.left[at : self.columns, :], self.right[:, cols], preferred_element_type=F32
            )
            out[at : self.columns, cols] = (
                base_coefficient * base[at : self.columns, cols] + coefficient * value
            )
            if to < self.wide:
                out[cols, to:] = out[to:, cols].T

    def newton(self, step):
        gram = self.gram[...]
        self.set_left(gram)
        self.set_right(gram)
        self.product(self.poly, COEF_C, self.gram, COEF_B)
        self.set_right(self.poly[...])
        value = self.iterate[...]
        high, low = split(value)
        self.iterate[...] = COEF_A * value + jnp.dot(
            jnp.concatenate([high, high, low], axis=1), self.right[...], preferred_element_type=F32
        )
        if step < ITERS - 1:
            self.product(self.inner, 1.0, self.gram, COEF_A)
            self.set_left(self.poly[...])
            self.set_right(self.inner[...])
            self.product(self.gram, 1.0, self.inner, COEF_A)

    def finish(self):
        update = self.gain * self.iterate[:, : self.columns]
        self.rows[...] = (self.old[...].astype(F32) * (1.0 - RATE * DECAY) - RATE * update).astype(BF16)
        self.update[...] = update

    def spread(self, near, far):
        self.first = []
        for side, target in enumerate((near, far)):
            copy = remote(
                self.rows, self.out_weight.at[self.d], self.ag_send.at[side], self.ag_recv.at[side], target
            )
            copy.start()
            self.first.append(copy)
        for i, (src, dst) in enumerate(
            ((self.rows, self.out_weight.at[self.d]), (self.update, self.out_update))
        ):
            copy = pltpu.make_async_copy(src, dst, self.out_sem.at[1 + i])
            copy.start()
            self.outs.append(copy)

    def forward(self, near, far):
        count = self.rows.shape[0]
        cut = count // 2 // 16 * 16
        self.later = []
        for side, (source, target, start, size) in enumerate(
            ((near[0], far, 0, cut), (far[0], near, cut, count - cut))
        ):
            self.first[side].wait_recv()
            if size:
                out = self.out_weight
                spot = out.at[source] if size == count else out.at[source, pl.ds(start, size)]
                copy = remote(spot, spot, self.ag_send.at[2 + side], self.ag_recv.at[2 + side], target)
                copy.start()
                self.later.append(copy)

    def end(self):
        for copy in self.outs + self.later:
            copy.wait()
        for copy in self.first + self.sent:
            copy.wait_send()


def kernel(dp, mp, *refs):
    d, m = lax.axis_index("dp"), lax.axis_index("mp")
    core = lax.rem(m, 2)
    sibling = (d, m + 1 - 2 * core)
    group = [(lax.rem(d + r, dp), m) for r in range(1, dp)]
    line = [(d, lax.rem(m + 2 * r, mp)) for r in range(1, mp // 2)]
    near = (d + 1 - 2 * lax.rem(d, 2), m)
    far = (lax.rem(d + 2, dp), m)
    across = near[0] + 2 - 4 * (d // 2)
    place = (d, m, core, sibling, group, line, near, far, across)
    scratch = refs[12:]
    count = len(scratch) // 2
    a = Side(place, 0.2 * math.sqrt(D), *refs[0:3], *refs[6:9], scratch[:count])
    b = Side(place, 0.2 * math.sqrt(KEY_VALUE_ROWS), *refs[3:6], *refs[9:12], scratch[count:])
    b.load()
    a.load()
    greet([sibling] + group + line)
    b.scatter()
    b.scatter_sent()
    a.scatter()
    b.scatter_pairs()
    a.scatter_sent()
    a.scatter_pairs()
    b.local_gram()
    b.core_start()
    b.core_end()
    b.dp_start()
    a.local_gram()
    a.core_start()
    b.dp_end()
    b.line_start()
    a.core_end()
    a.dp_start()
    b.line_end()
    b.line_back()
    a.dp_end()
    a.line_start()
    b.arrived()
    b.dp_back()
    a.line_end()
    a.line_back()
    b.arrived()
    b.core_back()
    a.arrived()
    a.dp_back()
    b.arrived()
    b.unpack()
    b.newton(0)
    a.arrived()
    a.core_back()
    for step in range(1, ITERS):
        b.newton(step)
    b.finish()
    b.spread(near, far)
    a.arrived()
    a.unpack()
    for step in range(ITERS):
        a.newton(step)
    a.finish()
    a.spread(near, far)
    b.forward(near, far)
    a.forward(near, far)
    for side in (a, b):
        for way, *_ in side.ways:
            side.scattered[2, way].wait_send()
    a.end()
    b.end()


def scratch_of(dp, mp, rows, columns):
    zn = mp // 2
    wide = padded(columns)
    total = packed_rows(columns, dp * mp)
    half = total // 2
    quarter = half // dp
    part = quarter // zn
    vmem, sem = pltpu.VMEM, pltpu.SemaphoreType.DMA
    return [
        vmem((rows, columns), BF16),
        vmem((rows, columns), BF16),
        vmem((2, rows, columns), BF16),
        vmem((rows, columns), BF16),
        vmem((rows, columns), BF16),
        vmem((rows, columns), F32),
        vmem((rows, columns), BF16),
        vmem((rows, columns), F32),
        vmem((rows, columns), F32),
        vmem((rows, columns), BF16),
        vmem((rows, wide), F32),
        vmem((total, BLOCK), F32),
        vmem((half, BLOCK), F32),
        vmem((quarter, BLOCK), F32),
        vmem((part, BLOCK), F32),
        vmem((total, BLOCK), F32),
        vmem((dp - 1, quarter, BLOCK), F32),
        vmem((zn - 1, part, BLOCK), F32),
        vmem((wide, wide), F32),
        vmem((wide, wide), F32),
        vmem((wide, wide), F32),
        vmem((wide, 3 * wide), BF16),
        vmem((3 * wide, wide), BF16),
        sem((5,)),
        sem((3,)),
        sem((3, 2)),
        sem((3, 2)),
        sem((4,)),
        sem((4, dp - 1)),
        sem((4, zn - 1)),
        sem((4,)),
        sem((4,)),
    ]


def local(dp, mp, *args):
    (ra, ca), (rb, cb) = args[1].shape, args[4].shape
    hbm = pl.BlockSpec(memory_space=pl.ANY)
    shape = jax.ShapeDtypeStruct
    results = pl.pallas_call(
        functools.partial(kernel, dp, mp),
        out_shape=[
            shape((dp, ra, ca), BF16), shape((ra, ca), F32), shape((ra, ca), F32),
            shape((dp, rb, cb), BF16), shape((rb, cb), F32), shape((rb, cb), F32),
        ],
        in_specs=[hbm] * 6,
        out_specs=[hbm] * 6,
        scratch_shapes=scratch_of(dp, mp, ra, ca) + scratch_of(dp, mp, rb, cb),
        compiler_params=pltpu.CompilerParams(
            collective_id=0, has_side_effects=True, vmem_limit_bytes=56 * 2**20
        ),
    )(*args)
    return place_results(results)


def place_kernel(count, *refs):
    sem = refs[-1]
    loads, stores = [], []
    for src, dst, stage in zip(refs[:count], refs[count : 2 * count], refs[2 * count : 3 * count]):
        rows = src.shape[-2]
        if len(src.shape) == 3:
            views = [(k,) for k in range(src.shape[0])]
        else:
            pieces = 4 if rows % 64 == 0 else 2 if rows % 32 == 0 else 1
            size = rows // pieces
            views = [(pl.ds(k * size, size),) for k in range(pieces)]
        for view in views:
            k = len(loads)
            loads.append(pltpu.make_async_copy(src.at[view], stage.at[view], sem.at[0, k]))
            stores.append(pltpu.make_async_copy(stage.at[view], dst.at[view], sem.at[1, k]))
    for load in loads:
        load.start()
    for load, store in zip(loads, stores):
        load.wait()
        store.start()
    for store in stores:
        store.wait()


def place_results(results):
    count = len(results)
    hbm = pl.BlockSpec(memory_space=pl.ANY)
    return pl.pallas_call(
        functools.partial(place_kernel, count),
        out_shape=[jax.ShapeDtypeStruct(r.shape, r.dtype) for r in results],
        in_specs=[hbm] * count,
        out_specs=[hbm] * count,
        scratch_shapes=[pltpu.VMEM(r.shape, r.dtype) for r in results]
        + [pltpu.SemaphoreType.DMA((2, 4 * count))],
        compiler_params=pltpu.CompilerParams(vmem_limit_bytes=56 * 2**20),
    )(*results)


def solution(mesh):
    both = P(("dp", "mp"), None)
    grads = P("dp", None, "mp", None)
    weights = P(None, "mp", None)
    return jax.shard_map(
        functools.partial(local, mesh.shape["dp"], mesh.shape["mp"]),
        mesh=mesh,
        in_specs=(grads, both, both, grads, both, both),
        out_specs=(weights, both, both, weights, both, both),
        check_vma=False,
    )
```
